32 devices in a mesh: dp: 4 (over x, core), tensor: 8 (over z, y).
Axes of the slice: x: 2, y: 2, z: 4, core: 2. Of those that a mesh axis runs over, the one named last changes fastest.
Arguments:
- train_acts: bfloat16 [256, 64, 28672], P('dp', None, 'tensor'), may hold values from -6 to 6
- train_grads: bfloat16 [256, 64, 8192], P('dp', None, 'tensor'), may hold values from -6 to 6
- query_acts: bfloat16 [64, 64, 28672], P('dp', None, 'tensor'), may hold values from -6 to 6
- query_grads: bfloat16 [64, 64, 8192], P('dp', None, 'tensor'), may hold values from -6 to 6
- proj_in: bfloat16 [28672, 32], P('tensor'), may hold values from -0.03125 to 0.03125
- proj_out: bfloat16 [8192, 32], P('tensor'), may hold values from -0.0625 to 0.0625
- train_counts: int32 [256], P('dp'), may hold values from 16 to 64
- query_counts: int32 [64], P('dp'), may hold values from 16 to 64
Outputs:
- scores: float32 [64, 256], P('tensor', 'dp')
The draws below stay inside these ranges and needn't reach their ends.
All inputs are finite; a program needn't handle non-finite values.
Results may differ from the reference program's by a relative error of at most 0.0003.
Values sent between devices are 32-bit elements; how exact they have to be, the bound alone decides.
A program may use at most 192 MiB of HBM per device.

```python
import jax
import jax.numpy as jnp
from jax import lax

D = 8192
FF = 28672
RANK = 32
L = 64
NTRAIN = 256
NQUERY = 64


def shared_directions(key, salt, width):
    return jax.random.normal(jax.random.fold_in(key, salt), (8, width), jnp.float32)


def build_features(fluctuation, coeffs, directions, falloff):
    shared_part = jnp.zeros((coeffs.shape[0], directions.shape[1]), jnp.float32)
    for index in range(8):
        weight_now = 10.0 ** (-falloff * index)
        shared_part = shared_part + coeffs[:, index:index + 1] * weight_now * directions[index][None, :]
    return jnp.clip(fluctuation + shared_part[:, None, :], -6.0, 6.0).astype(jnp.bfloat16)


def draw_train_acts(key, part):
    directions = shared_directions(key, 101, FF)
    key = jax.random.fold_in(key, 1)
    noise_key, coeff_key = jax.random.split(key, 2)
    fluctuation = jax.random.normal(noise_key, (NTRAIN, L, FF), jnp.float32)
    coeffs = jax.random.normal(coeff_key, (NTRAIN, 8), jnp.float32)
    return build_features(fluctuation, coeffs, directions, 0.125)


def draw_query_acts(key, part):
    directions = shared_directions(key, 101, FF)
    key = jax.random.fold_in(key, 2)
    noise_key, coeff_key = jax.random.split(key, 2)
    fluctuation = jax.random.normal(noise_key, (NQUERY, L, FF), jnp.float32)
    coeffs = jax.random.normal(coeff_key, (NQUERY, 8), jnp.float32)
    return build_features(fluctuation, coeffs, directions, 0.125)


def draw_train_grads(key, part):
    directions = shared_directions(key, 202, D)
    key = jax.random.fold_in(key, 3)
    noise_key, coeff_key = jax.random.split(key, 2)
    fluctuation = jax.random.normal(noise_key, (NTRAIN, L, D), jnp.float32)
    coeffs = jax.random.normal(coeff_key, (NTRAIN, 8), jnp.float32)
    return build_features(fluctuation, coeffs, directions, 0.1)


def draw_query_grads(key, part):
    directions = shared_directions(key, 202, D)
    key = jax.random.fold_in(key, 4)
    noise_key, coeff_key = jax.random.split(key, 2)
    fluctuation = jax.random.normal(noise_key, (NQUERY, L, D), jnp.float32)
    coeffs = jax.random.normal(coeff_key, (NQUERY, 8), jnp.float32)
    return build_features(fluctuation, coeffs, directions, 0.1)


def set_ends(array, key, smallest, largest):
    longest = array.shape.index(max(array.shape))
    spots = []
    for shift in (0, 1):
        where = [jax.random.randint(jax.random.fold_in(key, axis), (), 0, length) for axis, length in enumerate(array.shape)]
        where[longest] = (where[longest] + shift) % array.shape[longest]
        spots.append(tuple(where))
    return array.at[spots[0]].set(smallest).at[spots[1]].set(largest)


def levels(key, shape, cuts, low, high):
    loudness = 1.0
    for position, parts in cuts:
        draws = jax.random.uniform(jax.random.fold_in(jax.random.fold_in(key, 6), position), (parts,), jnp.float32, low / len(cuts), high / len(cuts))
        loudness = loudness * jnp.repeat(jnp.exp(draws), shape[position] // parts).reshape((-1,) + (1,) * (len(shape) - 1 - position))
    return loudness


def scatter_about(own_key, extent, deviation, limit, cuts=(), held_as=jnp.bfloat16):
    values = deviation * jax.random.normal(own_key, extent, jnp.float32)
    if cuts:
        values = values * levels(own_key, extent, cuts, -0.22, 0.18)
    return jnp.clip(values, -limit, limit).astype(held_as)


def setup_inputs(seed: int = 0) -> dict:
    key_of = jax.random.split(jax.random.key(seed), 9)
    train_acts = draw_train_acts(jax.random.fold_in(key_of[8], 71), 0)
    train_grads = draw_train_grads(jax.random.fold_in(key_of[8], 71), 0)
    query_acts = draw_query_acts(jax.random.fold_in(key_of[8], 71), 0)
    query_grads = draw_query_grads(jax.random.fold_in(key_of[8], 71), 0)
    proj_in = scatter_about(key_of[4], (FF, RANK), FF ** -0.5, 0.03125, ((0, 8),))
    proj_out = scatter_about(key_of[5], (D, RANK), D ** -0.5, 0.0625, ((0, 8),))
    train_counts = set_ends(jax.random.randint(key_of[6], (NTRAIN,), L // 4, L + 1), jax.random.fold_in(key_of[6], 1), L // 4, L).astype(jnp.int32)
    query_counts = set_ends(jax.random.randint(key_of[7], (NQUERY,), L // 4, L + 1), jax.random.fold_in(key_of[7], 1), L // 4, L).astype(jnp.int32)
    return dict(train_acts=train_acts, train_grads=train_grads, query_acts=query_acts, query_grads=query_grads, proj_in=proj_in, proj_out=proj_out, train_counts=train_counts, query_counts=query_counts)


def make_sketches(acts, grads, counts, proj_in, proj_out):

    def one_sketch(items):
        act_rows, grad_rows, count = items
        xproj = jnp.dot(act_rows.astype(jnp.float32), proj_in.astype(jnp.float32), preferred_element_type=jnp.float32)
        gproj = jnp.dot(grad_rows.astype(jnp.float32), proj_out.astype(jnp.float32), preferred_element_type=jnp.float32)
        valid = (jnp.arange(act_rows.shape[0], dtype=jnp.int32) < count).astype(jnp.float32)
        gproj = gproj * valid[:, None]
        block = jnp.dot(gproj.T.astype(jnp.float32), xproj.astype(jnp.float32), precision=lax.Precision.HIGHEST, preferred_element_type=jnp.float32)
        return block.reshape(-1)
    return lax.map(one_sketch, (acts, grads, counts))

def reference(train_acts, train_grads, query_acts, query_grads, proj_in, proj_out, train_counts, query_counts):
    train_sketch = make_sketches(train_acts, train_grads, train_counts, proj_in, proj_out)
    query_sketch = make_sketches(query_acts, query_grads, query_counts, proj_in, proj_out)
    total = jnp.sum(train_counts.astype(jnp.float32))
    fisher = jnp.dot(train_sketch.T.astype(jnp.float32), train_sketch.astype(jnp.float32), precision=lax.Precision.HIGHEST, preferred_element_type=jnp.float32) / total
    width = fisher.shape[0]
    lam = 0.1 * jnp.trace(fisher) / width
    damped = fisher + lam * jnp.eye(width, dtype=jnp.float32)
    factor = jnp.linalg.cholesky(damped)
    pre = jax.scipy.linalg.cho_solve((factor, True), query_sketch.T)
    scores = jnp.dot(pre.T.astype(jnp.float32), train_sketch.T.astype(jnp.float32), precision=lax.Precision.HIGHEST, preferred_element_type=jnp.float32)
    return scores / NTRAIN
```

```python
import functools

import jax
import jax.numpy as jnp
from jax import lax
from jax.experimental import pallas as pl
from jax.experimental.pallas import tpu as pltpu
from jax.sharding import PartitionSpec as P

LANES = 128


def project_pair(acts, grads, proj_in, proj_out):
    xproj = jnp.einsum("stf,fr->srt", acts, proj_in, preferred_element_type=jnp.float32)
    gproj = jnp.einsum("std,dr->srt", grads, proj_out, preferred_element_type=jnp.float32)
    joined = jnp.concatenate([gproj, xproj], axis=1)
    return joined.reshape(joined.shape[0], -1)


def form_sketches(joined, counts, width, length):
    joined = joined.reshape(joined.shape[0], 2 * width, length)
    valid = (jnp.arange(length, dtype=jnp.int32)[None, :] < counts[:, None]).astype(jnp.float32)
    gproj = joined[:, :width, :] * valid[:, None, :]
    xproj = joined[:, width:, :]
    block = jnp.einsum(
        "sat,sbt->sab",
        gproj,
        xproj,
        precision=lax.Precision.HIGHEST,
        preferred_element_type=jnp.float32,
    )
    return block.reshape(block.shape[0], width * width)


def bcast_row(tile, i):
    return jnp.broadcast_to(tile[i : i + 1, :], tile.shape)


def lane_pick(tile, index):
    return jnp.take_along_axis(tile, index, axis=1, mode="promise_in_bounds")


def solve_kernel(rows_out, scale, s_ref, q_ref, cnt_ref, out_ref, wide, qwide, a_ref):
    n = a_ref.shape[0]
    nq = qwide.shape[0]
    parts = s_ref.shape[0] // n
    tiles = n // LANES
    dims = (((1,), (1,)), ((), ()))
    exact = dict(precision=lax.Precision.HIGHEST, preferred_element_type=jnp.float32)
    for r in range(parts):
        wide[:, r * LANES : (r + 1) * LANES] = s_ref[pl.ds(r, n, stride=parts), :]
        qwide[:, r * LANES : (r + 1) * LANES] = q_ref[pl.ds(r, nq, stride=parts), :]
    total = jnp.sum(cnt_ref[...])
    gram = lax.dot_general(wide[...], wide[...], dims, **exact)
    cross = lax.dot_general(qwide[...], wide[...], dims, **exact)
    diag = lax.broadcasted_iota(jnp.int32, (n, n), 0) == lax.broadcasted_iota(jnp.int32, (n, n), 1)
    lam = 0.1 * (jnp.sum(jnp.where(diag, gram, 0.0)) / total) / (parts * LANES)
    a_ref[...] = gram / total + jnp.where(diag, lam, 0.0)

    sub = lax.broadcasted_iota(jnp.int32, (8, LANES), 0)
    lane = lax.broadcasted_iota(jnp.int32, (8, LANES), 1)

    def block(kb, carry):
        k0 = pl.multiple_of(kb * 8, 8)
        kt = pl.multiple_of((k0 // LANES) * LANES, LANES)
        kl = k0 % LANES
        picks = [jnp.full((8, LANES), kl + i, jnp.int32) for i in range(8)]
        pivot = a_ref[pl.ds(k0, 8), pl.ds(kt, LANES)]
        cols = [lane_pick(pivot, picks[i]) for i in range(8)]
        inside, right = [], []
        for j in range(tiles):
            offset = lane + (j * LANES - k0)
            mask = (offset >= 0) & (offset < 8)
            inside.append(mask)
            row = a_ref[pl.ds(k0, 8), j * LANES : (j + 1) * LANES]
            right.append(jnp.where(mask, jnp.where(offset == sub, 1.0, 0.0), row))
        for i in range(8):
            own = sub == i
            inv = 1.0 / bcast_row(cols[i], i)
            factor = cols[i]
            for m in range(i + 1, 8):
                row = bcast_row(cols[m], i) * inv
                cols[m] = jnp.where(own, row, cols[m] - factor * row)
            for j in range(tiles):
                row = bcast_row(right[j], i) * inv
                right[j] = jnp.where(own, row, right[j] - factor * row)
        spread = [[bcast_row(right[j], i) for j in range(tiles)] for i in range(8)]
        for rt in range(n // 8):
            here = slice(rt * 8, rt * 8 + 8)
            column = a_ref[here, pl.ds(kt, LANES)]
            heads = [lane_pick(column, picks[i]) for i in range(8)]
            for j in range(tiles):
                there = slice(j * LANES, (j + 1) * LANES)
                value = jnp.where(inside[j], 0.0, a_ref[here, there])
                for i in range(8):
                    value = value - heads[i] * spread[i][j]
                a_ref[here, there] = value
        for j in range(tiles):
            a_ref[pl.ds(k0, 8), j * LANES : (j + 1) * LANES] = right[j]
        return carry

    lax.fori_loop(0, n // 8, block, 0)
    first = pl.multiple_of(lax.axis_index("dp") * rows_out, 8)
    out_ref[...] = lax.dot_general(cross, a_ref[pl.ds(first, rows_out), :], dims, **exact) / scale


def solve(train, query, counts, n, nq, rows_out):
    width = train.shape[0] * LANES // n
    return pl.pallas_call(
        functools.partial(solve_kernel, rows_out, n),
        out_shape=jax.ShapeDtypeStruct((nq, rows_out), jnp.float32),
        in_specs=[pl.BlockSpec(memory_space=pltpu.VMEM)] * 3,
        out_specs=pl.BlockSpec(memory_space=pltpu.VMEM),
        scratch_shapes=[
            pltpu.VMEM((n, width), jnp.float32),
            pltpu.VMEM((nq, width), jnp.float32),
            pltpu.VMEM((n, n), jnp.float32),
        ],
        compiler_params=pltpu.CompilerParams(vmem_limit_bytes=48 * 2**20),
    )(train, query, counts)


def local(
    train_acts, train_grads, query_acts, query_grads, proj_in, proj_out, train_counts, query_counts
):
    width = proj_in.shape[1]
    length = train_acts.shape[1]
    train_pair = project_pair(train_acts, train_grads, proj_in, proj_out)
    query_pair = lax.psum(project_pair(query_acts, query_grads, proj_in, proj_out), "tensor")
    query_sketch = form_sketches(query_pair, query_counts, width, length)
    every_query = lax.all_gather(query_sketch, "dp", axis=0, tiled=True)
    full_pair = lax.psum(train_pair, "tensor")
    local_train = form_sketches(full_pair, train_counts, width, length)
    every_train, every_count = (
        lax.all_gather(local_train, "dp", axis=0, tiled=True),
        lax.all_gather(train_counts, "dp", axis=0, tiled=True),
    )
    query_share = every_query.shape[0] // lax.axis_size("tensor")
    my_queries = lax.dynamic_slice_in_dim(
        every_query, lax.axis_index("tensor") * query_share, query_share
    )
    n = every_train.shape[0]
    return solve(
        every_train.reshape(-1, LANES),
        my_queries.reshape(-1, LANES),
        every_count.astype(jnp.float32).reshape(-1, LANES),
        n,
        query_share,
        local_train.shape[0],
    )


def solution(mesh):
    placed = (
        P("dp", None, "tensor"),
        P("dp", None, "tensor"),
        P("dp", None, "tensor"),
        P("dp", None, "tensor"),
        P("tensor", None),
        P("tensor", None),
        P("dp"),
        P("dp"),
    )
    return jax.shard_map(
        local, mesh=mesh, in_specs=placed, out_specs=P("tensor", "dp"), check_vma=False
    )
```

```python
import functools

import jax
import jax.numpy as jnp
from jax import lax
from jax.experimental import pallas as pl
from jax.experimental.pallas import tpu as pltpu
from jax.sharding import PartitionSpec as P

LANES = 128


def place(width, offset):
    row = lax.broadcasted_iota(jnp.int32, (width, LANES), 0)
    col = lax.broadcasted_iota(jnp.int32, (width, LANES), 1)
    return jnp.where(row + offset == col, 1.0, 0.0).astype(jnp.bfloat16)


def sketch_kernel(
    dps, outer, inner,
    tacts, tgrads, qacts, qgrads, pin, pout, tcount, qcount,
    train_out, query_out, count_out,
    abuf, gbuf, win, wout, yout, yin, own, zin, gath,
    load_sem, ysend, yrecv, zsend, zrecv, gzs, gzr, gys, gyr, gxs, gxr, gcs, gcr, out_sem,
):
    width = pin.shape[1]
    tensor = outer * inner
    nt, nq = tacts.shape[0] // tensor, qacts.shape[0] // tensor
    ns = nt + nq
    half = tacts.shape[1] // 2
    feat, model = pin.shape[0], pout.shape[0]
    chips = dps // 2
    dp, me = lax.axis_index("dp"), lax.axis_index("tensor")
    z, y = me // inner, me % inner
    x, core = dp // 2, dp % 2
    mesh_id = pl.DeviceIdType.MESH

    def at_z(k):
        return (dp, ((z + k) % outer) * inner + y)

    def at_y(k):
        return (dp, z * inner + (y + k) % inner)

    def at_x(k):
        return (((x + k) % chips) * 2 + core, me)

    sibling = (x * 2 + 1 - core, me)

    steps = [(zi, dy) for zi in range(outer) for dy in list(range(1, inner)) + [0]]
    slots = abuf.shape[0]

    def loads(step):
        zi, dy = steps[step]
        owner = ((z + 1 + zi) % outer) * inner + (y + dy) % inner
        slot = step % slots
        pairs = (
            (tacts.at[pl.ds(owner * nt, nt)], abuf.at[slot, pl.ds(0, nt)]),
            (tgrads.at[pl.ds(owner * nt, nt)], gbuf.at[slot, pl.ds(0, nt)]),
            (qacts.at[pl.ds(owner * nq, nq)], abuf.at[slot, pl.ds(nt, nq)]),
            (qgrads.at[pl.ds(owner * nq, nq)], gbuf.at[slot, pl.ds(nt, nq)]),
        )
        return [
            pltpu.make_async_copy(src, dst, load_sem.at[slot, i])
            for i, (src, dst) in enumerate(pairs)
        ]

    for step in range(min(slots, len(steps))):
        for copy in loads(step):
            copy.start()

    barrier = pltpu.get_barrier_semaphore()
    partners = [at_z(k) for k in range(1, outer)] + [at_y(k) for k in range(1, inner)]
    partners += [at_x(k) for k in range(1, chips)] + [sibling]
    for partner in partners:
        pl.semaphore_signal(barrier, inc=1, device_id=partner, device_id_type=mesh_id)

    for h in range(2):
        win[h] = jnp.dot(
            pin[...], place(width, 2 * width * h + width), preferred_element_type=jnp.float32
        ).astype(jnp.bfloat16)
        wout[h] = jnp.dot(
            pout[...], place(width, 2 * width * h), preferred_element_type=jnp.float32
        ).astype(jnp.bfloat16)
    pl.semaphore_wait(barrier, len(partners))

    def project(slot):
        total = None
        for h in range(2):
            rows = slice(h * half, (h + 1) * half)
            a = abuf[slot, :, rows, :].reshape(ns * half, feat)
            g = gbuf[slot, :, rows, :].reshape(ns * half, model)
            term = jnp.dot(a, win[h], preferred_element_type=jnp.float32)
            term = term + jnp.dot(g, wout[h], preferred_element_type=jnp.float32)
            total = term if total is None else total + term
        return total

    def remote(src, dst, send, recv, target):
        return pltpu.make_async_remote_copy(
            src_ref=src, dst_ref=dst, send_sem=send, recv_sem=recv,
            device_id=target, device_id_type=mesh_id,
        )

    ycopies, zcopies = {}, []

    def finish(zi):
        value = own[zi]
        for dy in range(1, inner):
            ycopies[zi, dy].wait_recv()
            value = value + yin[dy - 1, zi]
        own[zi] = value
        if zi < outer - 1:
            copy = remote(
                own.at[zi], zin.at[zi], zsend.at[zi], zrecv.at[zi], at_z(zi + 1)
            )
            copy.start()
            zcopies.append(copy)

    for step, (zi, dy) in enumerate(steps):
        for copy in loads(step):
            copy.wait()
        value = project(step % slots)
        if dy:
            yout[dy - 1, zi] = value
            copy = remote(
                yout.at[dy - 1, zi], yin.at[dy - 1, zi],
                ysend.at[dy - 1, zi], yrecv.at[dy - 1, zi], at_y(dy),
            )
            copy.start()
            ycopies[zi, dy] = copy
        else:
            own[zi] = value
        if step + slots < len(steps):
            for copy in loads(step + slots):
                copy.start()
        if dy == 0 and zi >= 1:
            finish(zi - 1)
    finish(outer - 1)

    full = own[outer - 1]
    for zi, copy in enumerate(zcopies):
        copy.wait_recv()
        full = full + zin[zi]

    row = lax.broadcasted_iota(jnp.int32, (half, LANES), 0)
    col = lax.broadcasted_iota(jnp.int32, (half, LANES), 1)
    token = row + jnp.where(col >= 2 * width, half, 0)
    group = lax.broadcasted_iota(jnp.int32, (8, LANES), 1) // width
    mine = dp * tensor + me
    count_sum = jnp.int32(0)
    for s in range(ns):
        if s < nt:
            count = tcount[me * nt + s]
            count_sum = count_sum + count
        else:
            count = qcount[me * nq + s - nt]
        joined = full[s * half : (s + 1) * half]
        masked = jnp.where(token < count, joined, 0.0)
        prod = lax.dot_general(
            masked, joined, (((0,), (0,)), ((), ())),
            precision=lax.Precision.HIGHEST, preferred_element_type=jnp.float32,
        )
        tile = jnp.zeros((8, LANES), jnp.float32)
        for q in range(width // 8):
            first = prod[q * 8 : q * 8 + 8]
            second = prod[2 * width + q * 8 : 2 * width + q * 8 + 8]
            first = pltpu.roll(first, (q * width - width) % LANES, 1)
            second = pltpu.roll(second, (q * width - 3 * width) % LANES, 1)
            tile = jnp.where(group == q, first + second, tile)
        gath[mine, s * 8 : s * 8 + 8, :] = tile
    corner = (lax.broadcasted_iota(jnp.int32, (8, LANES), 0) == 0) & (
        lax.broadcasted_iota(jnp.int32, (8, LANES), 1) == 0
    )
    gath[mine, ns * 8 : ns * 8 + 8, :] = jnp.where(corner, count_sum.astype(jnp.float32), 0.0)

    sends = []

    def share(block, send, recv, target):
        copy = remote(block, block, send, recv, target)
        copy.start()
        sends.append(copy)
        return copy

    zs = [share(gath.at[mine], gzs.at[k - 1], gzr.at[k - 1], at_z(k)) for k in range(1, outer)]
    ys = []
    for j in range(outer):
        if j:
            zs[j - 1].wait_recv()
        block = gath.at[dp * tensor + ((z - j + outer) % outer) * inner + y]
        for k in range(1, inner):
            ys.append(share(block, gys.at[k - 1, j], gyr.at[k - 1, j], at_y(k)))
    for copy in ys:
        copy.wait_recv()
    block = gath.at[pl.ds(dp * tensor, tensor)]
    xs = [share(block, gxs.at[k - 1], gxr.at[k - 1], at_x(k)) for k in range(1, chips)]
    cs = []
    for j in range(chips):
        if j:
            xs[j - 1].wait_recv()
        block = gath.at[pl.ds((((x - j + chips) % chips) * 2 + core) * tensor, tensor)]
        cs.append(share(block, gcs.at[j], gcr.at[j], sibling))
    for copy in cs:
        copy.wait_recv()
    finals = [
        pltpu.make_async_copy(gath.at[:, pl.ds(0, nt * 8)], train_out, out_sem.at[0]),
        pltpu.make_async_copy(
            gath.at[pl.ds(me * dps, dps), pl.ds(nt * 8, nq * 8)], query_out, out_sem.at[1]
        ),
        pltpu.make_async_copy(gath.at[:, pl.ds(ns * 8, 8)], count_out, out_sem.at[2]),
    ]
    for copy in finals:
        copy.start()
    for copy in list(ycopies.values()) + zcopies + sends:
        copy.wait_send()
    for copy in finals:
        copy.wait()


def sketches(dps, tensor, tacts, tgrads, qacts, qgrads, pin, pout, tcount, qcount):
    outer = 4 if tensor % 4 == 0 else 1
    inner = tensor // outer
    chips = dps // 2
    nt, nq = tacts.shape[0] // tensor, qacts.shape[0] // tensor
    ns = nt + nq
    length, feat, model = tacts.shape[1], tacts.shape[2], tgrads.shape[2]
    devices = dps * tensor
    slots = 3
    f32 = jnp.float32
    block = (ns * length // 2, LANES)
    many = lambda *shape: pltpu.SemaphoreType.DMA(tuple(max(1, n) for n in shape))
    anywhere, vmem = pl.BlockSpec(memory_space=pl.ANY), pl.BlockSpec(memory_space=pltpu.VMEM)
    smem = pl.BlockSpec(memory_space=pltpu.SMEM)
    return pl.pallas_call(
        functools.partial(sketch_kernel, dps, outer, inner),
        out_shape=(
            jax.ShapeDtypeStruct((devices, nt * 8, LANES), f32),
            jax.ShapeDtypeStruct((dps, nq * 8, LANES), f32),
            jax.ShapeDtypeStruct((devices, 8, LANES), f32),
        ),
        in_specs=[anywhere] * 4 + [vmem] * 2 + [smem] * 2,
        out_specs=(anywhere,) * 3,
        scratch_shapes=[
            pltpu.VMEM((slots, ns, length, feat), jnp.bfloat16),
            pltpu.VMEM((slots, ns, length, model), jnp.bfloat16),
            pltpu.VMEM((2, feat, LANES), jnp.bfloat16),
            pltpu.VMEM((2, model, LANES), jnp.bfloat16),
            pltpu.VMEM((max(1, inner - 1), outer) + block, f32),
            pltpu.VMEM((max(1, inner - 1), outer) + block, f32),
            pltpu.VMEM((outer,) + block, f32),
            pltpu.VMEM((max(1, outer - 1),) + block, f32),
            pltpu.VMEM((devices, ns * 8 + 8, LANES), f32),
            many(slots, 4),
            many(inner - 1, outer), many(inner - 1, outer),
            many(outer - 1), many(outer - 1),
            many(outer - 1), many(outer - 1),
            many(inner - 1, outer), many(inner - 1, outer),
            many(chips - 1), many(chips - 1),
            many(chips), many(chips),
            many(3),
        ],
        compiler_params=pltpu.CompilerParams(
            collective_id=0, has_side_effects=True, vmem_limit_bytes=56 * 2**20
        ),
    )(tacts, tgrads, qacts, qgrads, pin, pout, tcount, qcount)


def bcast_row(tile, i):
    return jnp.broadcast_to(tile[i : i + 1, :], tile.shape)


def lane_pick(tile, index):
    return jnp.take_along_axis(tile, index, axis=1, mode="promise_in_bounds")


def solve_kernel(rows_out, scale, s_ref, q_ref, cnt_ref, out_ref, wide, qwide, a_ref):
    n = a_ref.shape[0]
    nq = qwide.shape[0]
    parts = s_ref.shape[0] // n
    tiles = n // LANES
    dims = (((1,), (1,)), ((), ()))
    exact = dict(precision=lax.Precision.HIGHEST, preferred_element_type=jnp.float32)
    for r in range(parts):
        wide[:, r * LANES : (r + 1) * LANES] = s_ref[pl.ds(r, n, stride=parts), :]
        qwide[:, r * LANES : (r + 1) * LANES] = q_ref[pl.ds(r, nq, stride=parts), :]
    total = jnp.sum(cnt_ref[...])
    gram = lax.dot_general(wide[...], wide[...], dims, **exact)
    cross = lax.dot_general(qwide[...], wide[...], dims, **exact)
    diag = lax.broadcasted_iota(jnp.int32, (n, n), 0) == lax.broadcasted_iota(jnp.int32, (n, n), 1)
    lam = 0.1 * (jnp.sum(jnp.where(diag, gram, 0.0)) / total) / (parts * LANES)
    a_ref[...] = gram / total + jnp.where(diag, lam, 0.0)

    sub = lax.broadcasted_iota(jnp.int32, (8, LANES), 0)
    lane = lax.broadcasted_iota(jnp.int32, (8, LANES), 1)

    def block(kb, carry):
        k0 = pl.multiple_of(kb * 8, 8)
        kt = pl.multiple_of((k0 // LANES) * LANES, LANES)
        kl = k0 % LANES
        picks = [jnp.full((8, LANES), kl + i, jnp.int32) for i in range(8)]
        pivot = a_ref[pl.ds(k0, 8), pl.ds(kt, LANES)]
        cols = [lane_pick(pivot, picks[i]) for i in range(8)]
        inside, right = [], []
        for j in range(tiles):
            offset = lane + (j * LANES - k0)
            mask = (offset >= 0) & (offset < 8)
            inside.append(mask)
            row = a_ref[pl.ds(k0, 8), j * LANES : (j + 1) * LANES]
            right.append(jnp.where(mask, jnp.where(offset == sub, 1.0, 0.0), row))
        for i in range(8):
            own = sub == i
            inv = 1.0 / bcast_row(cols[i], i)
            factor = cols[i]
            for m in range(i + 1, 8):
                row = bcast_row(cols[m], i) * inv
                cols[m] = jnp.where(own, row, cols[m] - factor * row)
            for j in range(tiles):
                row = bcast_row(right[j], i) * inv
                right[j] = jnp.where(own, row, right[j] - factor * row)
        spread = [[bcast_row(right[j], i) for j in range(tiles)] for i in range(8)]
        for rt in range(n // 8):
            here = slice(rt * 8, rt * 8 + 8)
            column = a_ref[here, pl.ds(kt, LANES)]
            heads = [lane_pick(column, picks[i]) for i in range(8)]
            for j in range(tiles):
                there = slice(j * LANES, (j + 1) * LANES)
                value = jnp.where(inside[j], 0.0, a_ref[here, there])
                for i in range(8):
                    value = value - heads[i] * spread[i][j]
                a_ref[here, there] = value
        for j in range(tiles):
            a_ref[pl.ds(k0, 8), j * LANES : (j + 1) * LANES] = right[j]
        return carry

    lax.fori_loop(0, n // 8, block, 0)
    first = pl.multiple_of(lax.axis_index("dp") * rows_out, 8)
    out_ref[...] = lax.dot_general(cross, a_ref[pl.ds(first, rows_out), :], dims, **exact) / scale


def solve(train, query, counts, n, nq, rows_out):
    width = train.shape[0] * LANES // n
    return pl.pallas_call(
        functools.partial(solve_kernel, rows_out, n),
        out_shape=jax.ShapeDtypeStruct((nq, rows_out), jnp.float32),
        in_specs=[pl.BlockSpec(memory_space=pltpu.VMEM)] * 3,
        out_specs=pl.BlockSpec(memory_space=pltpu.VMEM),
        scratch_shapes=[
            pltpu.VMEM((n, width), jnp.float32),
            pltpu.VMEM((nq, width), jnp.float32),
            pltpu.VMEM((n, n), jnp.float32),
        ],
        compiler_params=pltpu.CompilerParams(vmem_limit_bytes=48 * 2**20),
    )(train, query, counts)


def local(
    train_acts, train_grads, query_acts, query_grads, proj_in, proj_out, train_counts, query_counts
):
    dps, tensor = lax.axis_size("dp"), lax.axis_size("tensor")
    train, query, counts = sketches(
        dps, tensor, train_acts, train_grads, query_acts, query_grads,
        proj_in, proj_out, train_counts, query_counts,
    )
    return solve(
        train.reshape(-1, LANES),
        query.reshape(-1, LANES),
        counts.reshape(-1, LANES),
        train_acts.shape[0] * dps,
        query_acts.shape[0] * dps // tensor,
        train_acts.shape[0],
    )


def solution(mesh):
    placed = (
        P("dp", None, "tensor"),
        P("dp", None, "tensor"),
        P("dp", None, "tensor"),
        P("dp", None, "tensor"),
        P("tensor", None),
        P("tensor", None),
        P("dp"),
        P("dp"),
    )
    return jax.shard_map(
        local, mesh=mesh, in_specs=placed, out_specs=P("tensor", "dp"), check_vma=False
    )
```

```python
import functools

import jax
import jax.numpy as jnp
from jax import lax
from jax.experimental import pallas as pl
from jax.experimental.pallas import tpu as pltpu
from jax.sharding import PartitionSpec as P

LANES = 128
PANEL = 32


def place(width, offset):
    row = lax.broadcasted_iota(jnp.int32, (width, LANES), 0)
    col = lax.broadcasted_iota(jnp.int32, (width, LANES), 1)
    return jnp.where(row + offset == col, 1.0, 0.0).astype(jnp.bfloat16)


def sketch_kernel(
    dps, outer, inner,
    tacts, tgrads, qacts, qgrads, pin, pout, tcount, qcount,
    train_out, query_out, count_out,
    abuf, gbuf, win, wout, yout, yin, own, zin, gath,
    load_sem, ysend, yrecv, zsend, zrecv, gzs, gzr, gys, gyr, gxs, gxr, gcs, gcr, out_sem,
):
    width = pin.shape[1]
    tensor = outer * inner
    nt, nq = tacts.shape[0] // tensor, qacts.shape[0] // tensor
    ns = nt + nq
    half = tacts.shape[1] // 2
    feat, model = pin.shape[0], pout.shape[0]
    chips = dps // 2
    dp, me = lax.axis_index("dp"), lax.axis_index("tensor")
    z, y = me // inner, me % inner
    x, core = dp // 2, dp % 2
    mesh_id = pl.DeviceIdType.MESH

    def at_z(k):
        return (dp, ((z + k) % outer) * inner + y)

    def at_y(k):
        return (dp, z * inner + (y + k) % inner)

    def at_x(k):
        return (((x + k) % chips) * 2 + core, me)

    sibling = (x * 2 + 1 - core, me)

    steps = [(zi, dy) for zi in range(outer) for dy in list(range(1, inner)) + [0]]
    slots = abuf.shape[0]

    def loads(step):
        zi, dy = steps[step]
        owner = ((z + 1 + zi) % outer) * inner + (y + dy) % inner
        slot = step % slots
        pairs = (
            (tacts.at[pl.ds(owner * nt, nt)], abuf.at[slot, pl.ds(0, nt)]),
            (tgrads.at[pl.ds(owner * nt, nt)], gbuf.at[slot, pl.ds(0, nt)]),
            (qacts.at[pl.ds(owner * nq, nq)], abuf.at[slot, pl.ds(nt, nq)]),
            (qgrads.at[pl.ds(owner * nq, nq)], gbuf.at[slot, pl.ds(nt, nq)]),
        )
        return [
            pltpu.make_async_copy(src, dst, load_sem.at[slot, i])
            for i, (src, dst) in enumerate(pairs)
        ]

    for step in range(min(slots, len(steps))):
        for copy in loads(step):
            copy.start()

    barrier = pltpu.get_barrier_semaphore()
    partners = [at_z(k) for k in range(1, outer)] + [at_y(k) for k in range(1, inner)]
    partners += [at_x(k) for k in range(1, chips)] + [sibling]
    for partner in partners:
        pl.semaphore_signal(barrier, inc=1, device_id=partner, device_id_type=mesh_id)

    for h in range(2):
        win[h] = jnp.dot(
            pin[...], place(width, 2 * width * h + width), preferred_element_type=jnp.float32
        ).astype(jnp.bfloat16)
        wout[h] = jnp.dot(
            pout[...], place(width, 2 * width * h), preferred_element_type=jnp.float32
        ).astype(jnp.bfloat16)
    pl.semaphore_wait(barrier, len(partners))

    def project(slot):
        total = None
        for h in range(2):
            rows = slice(h * half, (h + 1) * half)
            a = abuf[slot, :, rows, :].reshape(ns * half, feat)
            g = gbuf[slot, :, rows, :].reshape(ns * half, model)
            term = jnp.dot(a, win[h], preferred_element_type=jnp.float32)
            term = term + jnp.dot(g, wout[h], preferred_element_type=jnp.float32)
            total = term if total is None else total + term
        return total

    def remote(src, dst, send, recv, target):
        return pltpu.make_async_remote_copy(
            src_ref=src, dst_ref=dst, send_sem=send, recv_sem=recv,
            device_id=target, device_id_type=mesh_id,
        )

    ycopies, zcopies = {}, []

    def finish(zi):
        value = own[zi]
        for dy in range(1, inner):
            ycopies[zi, dy].wait_recv()
            value = value + yin[dy - 1, zi]
        own[zi] = value
        if zi < outer - 1:
            copy = remote(
                own.at[zi], zin.at[zi], zsend.at[zi], zrecv.at[zi], at_z(zi + 1)
            )
            copy.start()
            zcopies.append(copy)

    for step, (zi, dy) in enumerate(steps):
        for copy in loads(step):
            copy.wait()
        value = project(step % slots)
        if dy:
            yout[dy - 1, zi] = value
            copy = remote(
                yout.at[dy - 1, zi], yin.at[dy - 1, zi],
                ysend.at[dy - 1, zi], yrecv.at[dy - 1, zi], at_y(dy),
            )
            copy.start()
            ycopies[zi, dy] = copy
        else:
            own[zi] = value
        if step + slots < len(steps):
            for copy in loads(step + slots):
                copy.start()
        if dy == 0 and zi >= 1:
            finish(zi - 1)
    finish(outer - 1)

    full = own[outer - 1]
    for zi, copy in enumerate(zcopies):
        copy.wait_recv()
        full = full + zin[zi]

    row = lax.broadcasted_iota(jnp.int32, (half, LANES), 0)
    col = lax.broadcasted_iota(jnp.int32, (half, LANES), 1)
    token = row + jnp.where(col >= 2 * width, half, 0)
    group = lax.broadcasted_iota(jnp.int32, (8, LANES), 1) // width
    mine = dp * tensor + me
    count_sum = jnp.int32(0)
    for s in range(ns):
        if s < nt:
            count = tcount[me * nt + s]
            count_sum = count_sum + count
        else:
            count = qcount[me * nq + s - nt]
        joined = full[s * half : (s + 1) * half]
        masked = jnp.where(token < count, joined, 0.0)
        prod = lax.dot_general(
            masked, joined, (((0,), (0,)), ((), ())),
            precision=lax.Precision.HIGHEST, preferred_element_type=jnp.float32,
        )
        tile = jnp.zeros((8, LANES), jnp.float32)
        for q in range(width // 8):
            first = prod[q * 8 : q * 8 + 8]
            second = prod[2 * width + q * 8 : 2 * width + q * 8 + 8]
            first = pltpu.roll(first, (q * width - width) % LANES, 1)
            second = pltpu.roll(second, (q * width - 3 * width) % LANES, 1)
            tile = jnp.where(group == q, first + second, tile)
        gath[mine, s * 8 : s * 8 + 8, :] = tile
    corner = (lax.broadcasted_iota(jnp.int32, (8, LANES), 0) == 0) & (
        lax.broadcasted_iota(jnp.int32, (8, LANES), 1) == 0
    )
    gath[mine, ns * 8 : ns * 8 + 8, :] = jnp.where(corner, count_sum.astype(jnp.float32), 0.0)

    sends = []

    def share(block, send, recv, target):
        copy = remote(block, block, send, recv, target)
        copy.start()
        sends.append(copy)
        return copy

    zs = [share(gath.at[mine], gzs.at[k - 1], gzr.at[k - 1], at_z(k)) for k in range(1, outer)]
    ys = []
    for j in range(outer):
        if j:
            zs[j - 1].wait_recv()
        block = gath.at[dp * tensor + ((z - j + outer) % outer) * inner + y]
        for k in range(1, inner):
            ys.append(share(block, gys.at[k - 1, j], gyr.at[k - 1, j], at_y(k)))
    for copy in ys:
        copy.wait_recv()
    block = gath.at[pl.ds(dp * tensor, tensor)]
    xs = [share(block, gxs.at[k - 1], gxr.at[k - 1], at_x(k)) for k in range(1, chips)]
    cs = []
    for j in range(chips):
        if j:
            xs[j - 1].wait_recv()
        block = gath.at[pl.ds((((x - j + chips) % chips) * 2 + core) * tensor, tensor)]
        cs.append(share(block, gcs.at[j], gcr.at[j], sibling))
    for copy in cs:
        copy.wait_recv()
    finals = [
        pltpu.make_async_copy(gath.at[:, pl.ds(0, nt * 8)], train_out, out_sem.at[0]),
        pltpu.make_async_copy(
            gath.at[pl.ds(me * dps, dps), pl.ds(nt * 8, nq * 8)], query_out, out_sem.at[1]
        ),
        pltpu.make_async_copy(gath.at[:, pl.ds(ns * 8, 8)], count_out, out_sem.at[2]),
    ]
    for copy in finals:
        copy.start()
    for copy in list(ycopies.values()) + zcopies + sends:
        copy.wait_send()
    for copy in finals:
        copy.wait()


def sketches(dps, tensor, tacts, tgrads, qacts, qgrads, pin, pout, tcount, qcount):
    outer = 4 if tensor % 4 == 0 else 1
    inner = tensor // outer
    chips = dps // 2
    nt, nq = tacts.shape[0] // tensor, qacts.shape[0] // tensor
    ns = nt + nq
    length, feat, model = tacts.shape[1], tacts.shape[2], tgrads.shape[2]
    devices = dps * tensor
    slots = 3
    f32 = jnp.float32
    block = (ns * length // 2, LANES)
    many = lambda *shape: pltpu.SemaphoreType.DMA(tuple(max(1, n) for n in shape))
    anywhere, vmem = pl.BlockSpec(memory_space=pl.ANY), pl.BlockSpec(memory_space=pltpu.VMEM)
    smem = pl.BlockSpec(memory_space=pltpu.SMEM)
    return pl.pallas_call(
        functools.partial(sketch_kernel, dps, outer, inner),
        out_shape=(
            jax.ShapeDtypeStruct((devices, nt * 8, LANES), f32),
            jax.ShapeDtypeStruct((dps, nq * 8, LANES), f32),
            jax.ShapeDtypeStruct((devices, 8, LANES), f32),
        ),
        in_specs=[anywhere] * 4 + [vmem] * 2 + [smem] * 2,
        out_specs=(anywhere,) * 3,
        scratch_shapes=[
            pltpu.VMEM((slots, ns, length, feat), jnp.bfloat16),
            pltpu.VMEM((slots, ns, length, model), jnp.bfloat16),
            pltpu.VMEM((2, feat, LANES), jnp.bfloat16),
            pltpu.VMEM((2, model, LANES), jnp.bfloat16),
            pltpu.VMEM((max(1, inner - 1), outer) + block, f32),
            pltpu.VMEM((max(1, inner - 1), outer) + block, f32),
            pltpu.VMEM((outer,) + block, f32),
            pltpu.VMEM((max(1, outer - 1),) + block, f32),
            pltpu.VMEM((devices, ns * 8 + 8, LANES), f32),
            many(slots, 4),
            many(inner - 1, outer), many(inner - 1, outer),
            many(outer - 1), many(outer - 1),
            many(outer - 1), many(outer - 1),
            many(inner - 1, outer), many(inner - 1, outer),
            many(chips - 1), many(chips - 1),
            many(chips), many(chips),
            many(3),
        ],
        compiler_params=pltpu.CompilerParams(
            collective_id=0, has_side_effects=True, vmem_limit_bytes=56 * 2**20
        ),
    )(tacts, tgrads, qacts, qgrads, pin, pout, tcount, qcount)


def bcast_row(tile, i):
    return jnp.broadcast_to(tile[i : i + 1, :], tile.shape)


def lane_pick(tile, index):
    return jnp.take_along_axis(tile, index, axis=1, mode="promise_in_bounds")


def solve_kernel(rows_out, scale, s_ref, q_ref, cnt_ref, out_ref, wide, qwide, a_ref, panel, wpad):
    n = a_ref.shape[0]
    nq = qwide.shape[0]
    parts = s_ref.shape[0] // n
    tiles = n // LANES
    dims = (((1,), (1,)), ((), ()))
    exact = dict(precision=lax.Precision.HIGHEST, preferred_element_type=jnp.float32)
    for r in range(parts):
        wide[:, r * LANES : (r + 1) * LANES] = s_ref[pl.ds(r, n, stride=parts), :]
        qwide[:, r * LANES : (r + 1) * LANES] = q_ref[pl.ds(r, nq, stride=parts), :]
    total = jnp.sum(cnt_ref[...])
    gram = lax.dot_general(wide[...], wide[...], dims, **exact)
    cross = lax.dot_general(qwide[...], wide[...], dims, **exact)
    diag = lax.broadcasted_iota(jnp.int32, (n, n), 0) == lax.broadcasted_iota(jnp.int32, (n, n), 1)
    lam = 0.1 * (jnp.sum(jnp.where(diag, gram, 0.0)) / total) / (parts * LANES)
    a_ref[...] = gram / total + jnp.where(diag, lam, 0.0)

    sub = lax.broadcasted_iota(jnp.int32, (8, LANES), 0)
    lane = lax.broadcasted_iota(jnp.int32, (8, LANES), 1)

    wpad[...] = jnp.zeros_like(wpad)
    full_lane = lax.broadcasted_iota(jnp.int32, (n, n), 1)
    tile_lane = lax.broadcasted_iota(jnp.int32, (n, LANES), 1)

    def block(kb, carry):
        base = pl.multiple_of(kb * PANEL, PANEL)
        kt = pl.multiple_of((base // LANES) * LANES, LANES)
        kl = pl.multiple_of(base % LANES, PANEL)
        panel[...] = a_ref[pl.ds(base, PANEL), :]
        for sb in range(PANEL // 8):
            k0 = base + sb * 8
            mine = slice(sb * 8, sb * 8 + 8)
            picks = [jnp.full((8, LANES), kl + sb * 8 + i, jnp.int32) for i in range(8)]
            pivot = panel[mine, pl.ds(kt, LANES)]
            cols = [lane_pick(pivot, picks[i]) for i in range(8)]
            inside, right = [], []
            for j in range(tiles):
                offset = lane + (j * LANES - k0)
                mask = (offset >= 0) & (offset < 8)
                inside.append(mask)
                row = panel[mine, j * LANES : (j + 1) * LANES]
                right.append(jnp.where(mask, jnp.where(offset == sub, 1.0, 0.0), row))
            for i in range(8):
                here = sub == i
                inv = 1.0 / bcast_row(cols[i], i)
                factor = cols[i]
                for m in range(i + 1, 8):
                    row = bcast_row(cols[m], i) * inv
                    cols[m] = jnp.where(here, row, cols[m] - factor * row)
                for j in range(tiles):
                    row = bcast_row(right[j], i) * inv
                    right[j] = jnp.where(here, row, right[j] - factor * row)
            for rt in range(PANEL // 8):
                if rt == sb:
                    continue
                here = slice(rt * 8, rt * 8 + 8)
                column = panel[here, pl.ds(kt, LANES)]
                heads = [lane_pick(column, picks[i]) for i in range(8)]
                for j in range(tiles):
                    there = slice(j * LANES, (j + 1) * LANES)
                    value = jnp.where(inside[j], 0.0, panel[here, there])
                    for i in range(8):
                        value = value - heads[i] * bcast_row(right[j], i)
                    panel[here, there] = value
            for j in range(tiles):
                panel[mine, j * LANES : (j + 1) * LANES] = right[j]
        wpad[pl.ds(kl, PANEL), :] = panel[...]
        near = (tile_lane >= kl) & (tile_lane < kl + PANEL)
        column = jnp.where(near, a_ref[:, pl.ds(kt, LANES)], 0.0)
        drop = (full_lane >= base) & (full_lane < base + PANEL)
        a_ref[...] = jnp.where(drop, 0.0, a_ref[...]) - jnp.dot(column, wpad[...], **exact)
        a_ref[pl.ds(base, PANEL), :] = panel[...]
        return carry

    lax.fori_loop(0, n // PANEL, block, 0)
    first = pl.multiple_of(lax.axis_index("dp") * rows_out, 8)
    out_ref[...] = lax.dot_general(cross, a_ref[pl.ds(first, rows_out), :], dims, **exact) / scale


def solve(train, query, counts, n, nq, rows_out):
    width = train.shape[0] * LANES // n
    return pl.pallas_call(
        functools.partial(solve_kernel, rows_out, n),
        out_shape=jax.ShapeDtypeStruct((nq, rows_out), jnp.float32),
        in_specs=[pl.BlockSpec(memory_space=pltpu.VMEM)] * 3,
        out_specs=pl.BlockSpec(memory_space=pltpu.VMEM),
        scratch_shapes=[
            pltpu.VMEM((n, width), jnp.float32),
            pltpu.VMEM((nq, width), jnp.float32),
            pltpu.VMEM((n, n), jnp.float32),
            pltpu.VMEM((PANEL, n), jnp.float32),
            pltpu.VMEM((LANES, n), jnp.float32),
        ],
        compiler_params=pltpu.CompilerParams(vmem_limit_bytes=48 * 2**20),
    )(train, query, counts)


def local(
    train_acts, train_grads, query_acts, query_grads, proj_in, proj_out, train_counts, query_counts
):
    dps, tensor = lax.axis_size("dp"), lax.axis_size("tensor")
    train, query, counts = sketches(
        dps, tensor, train_acts, train_grads, query_acts, query_grads,
        proj_in, proj_out, train_counts, query_counts,
    )
    return solve(
        train.reshape(-1, LANES),
        query.reshape(-1, LANES),
        counts.reshape(-1, LANES),
        train_acts.shape[0] * dps,
        query_acts.shape[0] * dps // tensor,
        train_acts.shape[0],
    )


def solution(mesh):
    placed = (
        P("dp", None, "tensor"),
        P("dp", None, "tensor"),
        P("dp", None, "tensor"),
        P("dp", None, "tensor"),
        P("tensor", None),
        P("tensor", None),
        P("dp"),
        P("dp"),
    )
    return jax.shard_map(
        local, mesh=mesh, in_specs=placed, out_specs=P("tensor", "dp"), check_vma=False
    )
```

```python
import functools

import jax
import jax.numpy as jnp
from jax import lax
from jax.experimental import pallas as pl
from jax.experimental.pallas import tpu as pltpu
from jax.sharding import PartitionSpec as P

LANES = 128
PANEL = 32


def place(width, offset):
    row = lax.broadcasted_iota(jnp.int32, (width, LANES), 0)
    col = lax.broadcasted_iota(jnp.int32, (width, LANES), 1)
    return jnp.where(row + offset == col, 1.0, 0.0).astype(jnp.bfloat16)


def sketch_kernel(
    dps, outer, inner,
    tacts, tgrads, qacts, qgrads, pin, pout, tcount, qcount,
    train_out, query_out, count_out,
    abuf, gbuf, win, wout, yout, yin, own, zin, gath,
    load_sem, ysend, yrecv, zsend, zrecv, gzs, gzr, gys, gyr, gxs, gxr, gcs, gcr, out_sem,
):
    width = pin.shape[0]
    tensor = outer * inner
    nt, nq = tacts.shape[0] // tensor, qacts.shape[0] // tensor
    ns = nt + nq
    half = tacts.shape[1] // 2
    feat, model = pin.shape[1], pout.shape[1]
    chips = dps // 2
    dp, me = lax.axis_index("dp"), lax.axis_index("tensor")
    z, y = me // inner, me % inner
    x, core = dp // 2, dp % 2
    mesh_id = pl.DeviceIdType.MESH

    def at_z(k):
        return (dp, ((z + k) % outer) * inner + y)

    def at_y(k):
        return (dp, z * inner + (y + k) % inner)

    def at_x(k):
        return (((x + k) % chips) * 2 + core, me)

    sibling = (x * 2 + 1 - core, me)

    steps = [(zi, dy) for zi in range(outer) for dy in list(range(1, inner)) + [0]]
    slots = abuf.shape[0]

    def loads(step):
        zi, dy = steps[step]
        owner = ((z + 1 + zi) % outer) * inner + (y + dy) % inner
        slot = step % slots
        pairs = (
            (tacts.at[pl.ds(owner * nt, nt)], abuf.at[slot, pl.ds(0, nt)]),
            (tgrads.at[pl.ds(owner * nt, nt)], gbuf.at[slot, pl.ds(0, nt)]),
            (qacts.at[pl.ds(owner * nq, nq)], abuf.at[slot, pl.ds(nt, nq)]),
            (qgrads.at[pl.ds(owner * nq, nq)], gbuf.at[slot, pl.ds(nt, nq)]),
        )
        return [
            pltpu.make_async_copy(src, dst, load_sem.at[slot, i])
            for i, (src, dst) in enumerate(pairs)
        ]

    for step in range(min(slots, len(steps))):
        for copy in loads(step):
            copy.start()

    barrier = pltpu.get_barrier_semaphore()
    partners = [at_z(k) for k in range(1, outer)] + [at_y(k) for k in range(1, inner)]
    partners += [at_x(k) for k in range(1, chips)] + [sibling]
    for partner in partners:
        pl.semaphore_signal(barrier, inc=1, device_id=partner, device_id_type=mesh_id)

    for h in range(2):
        win[h] = lax.dot_general(
            pin[...], place(width, 2 * width * h + width), (((0,), (0,)), ((), ())),
            preferred_element_type=jnp.float32,
        ).astype(jnp.bfloat16)
        wout[h] = lax.dot_general(
            pout[...], place(width, 2 * width * h), (((0,), (0,)), ((), ())),
            preferred_element_type=jnp.float32,
        ).astype(jnp.bfloat16)
    pl.semaphore_wait(barrier, len(partners))

    def project(slot):
        total = None
        for h in range(2):
            rows = slice(h * half, (h + 1) * half)
            a = abuf[slot, :, rows, :].reshape(ns * half, feat)
            g = gbuf[slot, :, rows, :].reshape(ns * half, model)
            term = jnp.dot(a, win[h], preferred_element_type=jnp.float32)
            term = term + jnp.dot(g, wout[h], preferred_element_type=jnp.float32)
            total = term if total is None else total + term
        return total

    def remote(src, dst, send, recv, target):
        return pltpu.make_async_remote_copy(
            src_ref=src, dst_ref=dst, send_sem=send, recv_sem=recv,
            device_id=target, device_id_type=mesh_id,
        )

    ycopies, zcopies = {}, []

    def finish(zi):
        value = own[zi]
        for dy in range(1, inner):
            ycopies[zi, dy].wait_recv()
            value = value + yin[dy - 1, zi]
        own[zi] = value
        if zi < outer - 1:
            copy = remote(
                own.at[zi], zin.at[zi], zsend.at[zi], zrecv.at[zi], at_z(zi + 1)
            )
            copy.start()
            zcopies.append(copy)

    for step, (zi, dy) in enumerate(steps):
        for copy in loads(step):
            copy.wait()
        value = project(step % slots)
        if dy:
            yout[dy - 1, zi] = value
            copy = remote(
                yout.at[dy - 1, zi], yin.at[dy - 1, zi],
                ysend.at[dy - 1, zi], yrecv.at[dy - 1, zi], at_y(dy),
            )
            copy.start()
            ycopies[zi, dy] = copy
        else:
            own[zi] = value
        if step + slots < len(steps):
            for copy in loads(step + slots):
                copy.start()
        if dy == 0 and zi >= 1:
            finish(zi - 1)
    finish(outer - 1)

    full = own[outer - 1]
    for zi, copy in enumerate(zcopies):
        copy.wait_recv()
        full = full + zin[zi]

    row = lax.broadcasted_iota(jnp.int32, (half, LANES), 0)
    col = lax.broadcasted_iota(jnp.int32, (half, LANES), 1)
    token = row + jnp.where(col >= 2 * width, half, 0)
    group = lax.broadcasted_iota(jnp.int32, (8, LANES), 1) // width
    mine = dp * tensor + me
    count_sum = jnp.int32(0)
    for s in range(ns):
        if s < nt:
            count = tcount[me * nt + s]
            count_sum = count_sum + count
        else:
            count = qcount[me * nq + s - nt]
        joined = full[s * half : (s + 1) * half]
        masked = jnp.where(token < count, joined, 0.0)
        prod = lax.dot_general(
            masked, joined, (((0,), (0,)), ((), ())),
            precision=lax.Precision.HIGHEST, preferred_element_type=jnp.float32,
        )
        tile = jnp.zeros((8, LANES), jnp.float32)
        for q in range(width // 8):
            first = prod[q * 8 : q * 8 + 8]
            second = prod[2 * width + q * 8 : 2 * width + q * 8 + 8]
            first = pltpu.roll(first, (q * width - width) % LANES, 1)
            second = pltpu.roll(second, (q * width - 3 * width) % LANES, 1)
            tile = jnp.where(group == q, first + second, tile)
        gath[mine, s * 8 : s * 8 + 8, :] = tile
    corner = (lax.broadcasted_iota(jnp.int32, (8, LANES), 0) == 0) & (
        lax.broadcasted_iota(jnp.int32, (8, LANES), 1) == 0
    )
    gath[mine, ns * 8 : ns * 8 + 8, :] = jnp.where(corner, count_sum.astype(jnp.float32), 0.0)

    sends = []

    def share(block, send, recv, target):
        copy = remote(block, block, send, recv, target)
        copy.start()
        sends.append(copy)
        return copy

    zs = [share(gath.at[mine], gzs.at[k - 1], gzr.at[k - 1], at_z(k)) for k in range(1, outer)]
    ys, xs = {}, {}

    def share_x(j, k):
        slot = ((z - j + outer) % outer) * inner + (y - k + inner) % inner
        block = gath.at[dp * tensor + slot]
        order = j * inner + k
        for c in range(1, chips):
            xs[c, j, k] = share(block, gxs.at[c - 1, order], gxr.at[c - 1, order], at_x(c))

    for j in range(outer):
        if j:
            zs[j - 1].wait_recv()
        block = gath.at[dp * tensor + ((z - j + outer) % outer) * inner + y]
        for k in range(1, inner):
            ys[j, k] = share(block, gys.at[k - 1, j], gyr.at[k - 1, j], at_y(k))
        share_x(j, 0)
    for j in range(outer):
        for k in range(1, inner):
            ys[j, k].wait_recv()
            share_x(j, k)
    cs = []
    for c in range(chips):
        if c:
            for j in range(outer):
                for k in range(inner):
                    xs[c, j, k].wait_recv()
        block = gath.at[pl.ds((((x - c + chips) % chips) * 2 + core) * tensor, tensor)]
        cs.append(share(block, gcs.at[c], gcr.at[c], sibling))
    for copy in cs:
        copy.wait_recv()
    finals = [
        pltpu.make_async_copy(gath.at[:, pl.ds(0, nt * 8)], train_out, out_sem.at[0]),
        pltpu.make_async_copy(
            gath.at[pl.ds(me * dps, dps), pl.ds(nt * 8, nq * 8)], query_out, out_sem.at[1]
        ),
        pltpu.make_async_copy(gath.at[:, pl.ds(ns * 8, 8)], count_out, out_sem.at[2]),
    ]
    for copy in finals:
        copy.start()
    for copy in list(ycopies.values()) + zcopies + sends:
        copy.wait_send()
    for copy in finals:
        copy.wait()


def sketches(dps, tensor, tacts, tgrads, qacts, qgrads, pin, pout, tcount, qcount):
    outer = 4 if tensor % 4 == 0 else 1
    inner = tensor // outer
    chips = dps // 2
    nt, nq = tacts.shape[0] // tensor, qacts.shape[0] // tensor
    ns = nt + nq
    length, feat, model = tacts.shape[1], tacts.shape[2], tgrads.shape[2]
    devices = dps * tensor
    slots = 3
    f32 = jnp.float32
    block = (ns * length // 2, LANES)
    many = lambda *shape: pltpu.SemaphoreType.DMA(tuple(max(1, n) for n in shape))
    anywhere, vmem = pl.BlockSpec(memory_space=pl.ANY), pl.BlockSpec(memory_space=pltpu.VMEM)
    smem = pl.BlockSpec(memory_space=pltpu.SMEM)
    return pl.pallas_call(
        functools.partial(sketch_kernel, dps, outer, inner),
        out_shape=(
            jax.ShapeDtypeStruct((devices, nt * 8, LANES), f32),
            jax.ShapeDtypeStruct((dps, nq * 8, LANES), f32),
            jax.ShapeDtypeStruct((devices, 8, LANES), f32),
        ),
        in_specs=[anywhere] * 4 + [vmem] * 2 + [smem] * 2,
        out_specs=(anywhere,) * 3,
        scratch_shapes=[
            pltpu.VMEM((slots, ns, length, feat), jnp.bfloat16),
            pltpu.VMEM((slots, ns, length, model), jnp.bfloat16),
            pltpu.VMEM((2, feat, LANES), jnp.bfloat16),
            pltpu.VMEM((2, model, LANES), jnp.bfloat16),
            pltpu.VMEM((max(1, inner - 1), outer) + block, f32),
            pltpu.VMEM((max(1, inner - 1), outer) + block, f32),
            pltpu.VMEM((outer,) + block, f32),
            pltpu.VMEM((max(1, outer - 1),) + block, f32),
            pltpu.VMEM((devices, ns * 8 + 8, LANES), f32),
            many(slots, 4),
            many(inner - 1, outer), many(inner - 1, outer),
            many(outer - 1), many(outer - 1),
            many(outer - 1), many(outer - 1),
            many(inner - 1, outer), many(inner - 1, outer),
            many(chips - 1, tensor), many(chips - 1, tensor),
            many(chips), many(chips),
            many(3),
        ],
        compiler_params=pltpu.CompilerParams(
            collective_id=0, has_side_effects=True, vmem_limit_bytes=56 * 2**20
        ),
    )(tacts, tgrads, qacts, qgrads, pin, pout, tcount, qcount)


def bcast_row(tile, i):
    return jnp.broadcast_to(tile[i : i + 1, :], tile.shape)


def lane_pick(tile, index):
    return jnp.take_along_axis(tile, index, axis=1, mode="promise_in_bounds")


def solve_kernel(rows_out, scale, s_ref, q_ref, cnt_ref, out_ref, wide, qwide, a_ref, panel, wpad):
    n = a_ref.shape[0]
    nq = qwide.shape[0]
    parts = s_ref.shape[0] // n
    tiles = n // LANES
    dims = (((1,), (1,)), ((), ()))
    exact = dict(precision=lax.Precision.HIGHEST, preferred_element_type=jnp.float32)
    for r in range(parts):
        wide[:, r * LANES : (r + 1) * LANES] = s_ref[pl.ds(r, n, stride=parts), :]
        qwide[:, r * LANES : (r + 1) * LANES] = q_ref[pl.ds(r, nq, stride=parts), :]
    total = jnp.sum(cnt_ref[...])
    gram = lax.dot_general(wide[...], wide[...], dims, **exact)
    cross = lax.dot_general(qwide[...], wide[...], dims, **exact)
    diag = lax.broadcasted_iota(jnp.int32, (n, n), 0) == lax.broadcasted_iota(jnp.int32, (n, n), 1)
    lam = 0.1 * (jnp.sum(jnp.where(diag, gram, 0.0)) / total) / (parts * LANES)
    a_ref[...] = gram / total + jnp.where(diag, lam, 0.0)

    sub = lax.broadcasted_iota(jnp.int32, (8, LANES), 0)
    lane = lax.broadcasted_iota(jnp.int32, (8, LANES), 1)

    wpad[...] = jnp.zeros_like(wpad)
    full_lane = lax.broadcasted_iota(jnp.int32, (n, n), 1)
    tile_lane = lax.broadcasted_iota(jnp.int32, (n, LANES), 1)

    def block(kb, carry):
        base = pl.multiple_of(kb * PANEL, PANEL)
        kt = pl.multiple_of((base // LANES) * LANES, LANES)
        kl = pl.multiple_of(base % LANES, PANEL)
        panel[...] = a_ref[pl.ds(base, PANEL), :]
        for sb in range(PANEL // 8):
            k0 = base + sb * 8
            mine = slice(sb * 8, sb * 8 + 8)
            picks = [jnp.full((8, LANES), kl + sb * 8 + i, jnp.int32) for i in range(8)]
            pivot = panel[mine, pl.ds(kt, LANES)]
            cols = [lane_pick(pivot, picks[i]) for i in range(8)]
            inside, right = [], []
            for j in range(tiles):
                offset = lane + (j * LANES - k0)
                mask = (offset >= 0) & (offset < 8)
                inside.append(mask)
                row = panel[mine, j * LANES : (j + 1) * LANES]
                right.append(jnp.where(mask, jnp.where(offset == sub, 1.0, 0.0), row))
            for i in range(8):
                here = sub == i
                inv = 1.0 / bcast_row(cols[i], i)
                factor = cols[i]
                for m in range(i + 1, 8):
                    row = bcast_row(cols[m], i) * inv
                    cols[m] = jnp.where(here, row, cols[m] - factor * row)
                for j in range(tiles):
                    row = bcast_row(right[j], i) * inv
                    right[j] = jnp.where(here, row, right[j] - factor * row)
            for rt in range(PANEL // 8):
                if rt == sb:
                    continue
                here = slice(rt * 8, rt * 8 + 8)
                column = panel[here, pl.ds(kt, LANES)]
                heads = [lane_pick(column, picks[i]) for i in range(8)]
                for j in range(tiles):
                    there = slice(j * LANES, (j + 1) * LANES)
                    value = jnp.where(inside[j], 0.0, panel[here, there])
                    for i in range(8):
                        value = value - heads[i] * bcast_row(right[j], i)
                    panel[here, there] = value
            for j in range(tiles):
                panel[mine, j * LANES : (j + 1) * LANES] = right[j]
        wpad[pl.ds(kl, PANEL), :] = panel[...]
        near = (tile_lane >= kl) & (tile_lane < kl + PANEL)
        column = jnp.where(near, a_ref[:, pl.ds(kt, LANES)], 0.0)
        drop = (full_lane >= base) & (full_lane < base + PANEL)
        a_ref[...] = jnp.where(drop, 0.0, a_ref[...]) - jnp.dot(column, wpad[...], **exact)
        a_ref[pl.ds(base, PANEL), :] = panel[...]
        return carry

    lax.fori_loop(0, n // PANEL, block, 0)
    first = pl.multiple_of(lax.axis_index("dp") * rows_out, 8)
    out_ref[...] = lax.dot_general(cross, a_ref[pl.ds(first, rows_out), :], dims, **exact) / scale


def solve(train, query, counts, n, nq, rows_out):
    width = train.shape[0] * LANES // n
    return pl.pallas_call(
        functools.partial(solve_kernel, rows_out, n),
        out_shape=jax.ShapeDtypeStruct((nq, rows_out), jnp.float32),
        in_specs=[pl.BlockSpec(memory_space=pltpu.VMEM)] * 3,
        out_specs=pl.BlockSpec(memory_space=pltpu.VMEM),
        scratch_shapes=[
            pltpu.VMEM((n, width), jnp.float32),
            pltpu.VMEM((nq, width), jnp.float32),
            pltpu.VMEM((n, n), jnp.float32),
            pltpu.VMEM((PANEL, n), jnp.float32),
            pltpu.VMEM((LANES, n), jnp.float32),
        ],
        compiler_params=pltpu.CompilerParams(vmem_limit_bytes=48 * 2**20),
    )(train, query, counts)


def local(
    train_acts, train_grads, query_acts, query_grads, proj_in, proj_out, train_counts, query_counts
):
    dps, tensor = lax.axis_size("dp"), lax.axis_size("tensor")
    train, query, counts = sketches(
        dps, tensor, train_acts, train_grads, query_acts, query_grads,
        proj_in.T, proj_out.T, train_counts, query_counts,
    )
    return solve(
        train.reshape(-1, LANES),
        query.reshape(-1, LANES),
        counts.reshape(-1, LANES),
        train_acts.shape[0] * dps,
        query_acts.shape[0] * dps // tensor,
        train_acts.shape[0],
    )


def solution(mesh):
    placed = (
        P("dp", None, "tensor"),
        P("dp", None, "tensor"),
        P("dp", None, "tensor"),
        P("dp", None, "tensor"),
        P("tensor", None),
        P("tensor", None),
        P("dp"),
        P("dp"),
    )
    return jax.shard_map(
        local, mesh=mesh, in_specs=placed, out_specs=P("tensor", "dp"), check_vma=False
    )
```
